32 devices in a mesh: freq: 8 (over y, x, core), blk: 4 (over z).
Axes of the slice: x: 2, y: 2, z: 4, core: 2. Of those that a mesh axis runs over, the one named last changes fastest.
Arguments:
- voltages: bfloat16 [1024, 64, 2048], P('freq', 'blk'), may hold values from -6 to 6
- channel_order: int32 [512], replicated, may hold values from 0 to 511, each once
- owner_count: int32 [4], replicated, may hold values from 1 to 192, 512 in all
- channel_good: int32 [512], replicated, may hold values 0 or 1
Outputs:
- visibility: bfloat16 [2, 768, 1024, 640], P(None, 'blk', 'freq')
The draws below stay inside these ranges and needn't reach their ends.
Inputs may be any that keep to these rules, and one draw needn't show every extreme that they name: `channel_order`: every channel appears once. `owner_count`: the counts sum to 512; the largest is exactly 192.
All inputs are finite; a program needn't handle non-finite values.
Results may differ from the reference program's by a relative error of at most 0.0074.
Values may be sent and summed in bfloat16 or wider, within the bound.
A program may use at most 320 MiB of HBM per device.

```python
import math
import jax
import jax.numpy as jnp
import numpy as np
from jax import lax

NINP = 1024
NSAMP = 2048
NCH = 512
TAPS = 4
FRAMES = 64
BW = 128
HALF = 5
OWNERS = 4
CAP = 192
SLOTS = 768
CH0 = 256
N_FREQ = 8


def touch_ends(array, stream_key, least, top_value):
    shape = array.shape
    place = [jax.random.randint(jax.random.fold_in(stream_key, axis), (), 0, shape[axis]) for axis in range(len(shape))]
    array = array.at[tuple(place)].set(least)
    longest = shape.index(max(shape))
    place[longest] = (place[longest] + 1) % shape[longest]
    return array.at[tuple(place)].set(top_value)


def level_of(stream_key, shape, shards, smallest, largest):
    gain = 1.0
    for dim, parts in shards:
        draws = jax.random.uniform(jax.random.fold_in(jax.random.fold_in(stream_key, 6), dim), (parts,), jnp.float32, smallest / len(shards), largest / len(shards))
        gain = gain * jnp.repeat(jnp.exp(draws), shape[dim] // parts).reshape((-1,) + (1,) * (len(shape) - 1 - dim))
    return gain


def split_up(number_of, total, limit, lean):
    weights = [(1 << 20) // math.isqrt(standing ** lean) + 1 for standing in range(2, number_of + 1)]
    spare, given = total - limit - (number_of - 1), [1] * (number_of - 1)
    while spare > 0:
        free = [i for i in range(number_of - 1) if given[i] < limit]
        whole, remaining = sum([weights[i] for i in free]), spare
        for i in free:
            extra = min(limit - given[i], max(1, remaining * weights[i] // whole), spare)
            given[i] = given[i] + extra
            spare = spare - extra
    return np.array([limit] + given)


def ragged(own_key, amount, total, bound, lean):
    if amount == 2:
        one = jax.random.randint(own_key, (), max(1, total - bound), min(bound, total - 1) + 1)
        return jnp.stack([one, total - one])
    tallies = jnp.asarray(split_up(amount, total, bound, lean), jnp.int32)
    twos = (amount - 1) // 2
    source_of, taker = tallies[1:1 + 2 * twos:2], tallies[2:2 + 2 * twos:2]
    margin = jnp.minimum(source_of - 1, bound - taker)
    passed = jax.random.randint(jax.random.fold_in(own_key, 1), (twos,), 0, 1 << 20) % (margin + 1)
    tallies = tallies.at[1:1 + 2 * twos:2].set(source_of - passed).at[2:2 + 2 * twos:2].set(taker + passed)
    return tallies[jax.random.permutation(jax.random.fold_in(own_key, 2), amount)]


def gaussian(own_key, dims, deviation, limit, cuts=(), kind=jnp.bfloat16):
    drawn = jax.random.normal(own_key, dims, jnp.float32) * deviation
    if len(cuts) > 0:
        drawn = level_of(own_key, dims, cuts, -0.22, 0.18) * drawn
    return jnp.clip(drawn, min=-limit, max=limit).astype(kind)


def setup_inputs(seed: int = 0) -> dict:
    arg_keys = jax.random.split(jax.random.key(seed), 5)
    voltages = gaussian(arg_keys[0], (NINP, FRAMES, NSAMP), 1.0, 6.0, ((0, 8), (1, 4)))
    channel_order = jax.random.permutation(arg_keys[1], NCH).astype(jnp.int32)
    owner_count = ragged(arg_keys[2], OWNERS, NCH, CAP, 2).astype(jnp.int32)
    channel_good = touch_ends((jax.random.randint(arg_keys[3], (NCH,), 0, 8) < 7).astype(jnp.int32), jax.random.fold_in(arg_keys[3], 1), 0, 1)
    return dict(voltages=voltages, channel_order=channel_order, owner_count=owner_count, channel_good=channel_good)


def pfb_window():
    offsets_u = jnp.arange(TAPS * NSAMP, dtype=jnp.float32)
    centered = (offsets_u - TAPS * NSAMP / 2) / NSAMP
    hann_taper = 0.5 - 0.5 * jnp.cos(2 * jnp.pi * offsets_u / (TAPS * NSAMP))
    window = (jnp.sinc(centered) * hann_taper).reshape(TAPS, NSAMP)
    normalizer = 1.0 / jnp.sqrt(jnp.sum(window * window))
    return (window, normalizer)

def transform_table():
    sample = jnp.arange(NSAMP, dtype=jnp.int32)
    channel_id = CH0 + jnp.arange(NCH, dtype=jnp.int32)
    phases = sample[:, None] * channel_id[None, :] % NSAMP
    angles = 2 * jnp.pi / NSAMP * phases.astype(jnp.float32)
    return jnp.stack([jnp.cos(angles), -jnp.sin(angles)], axis=2).astype(jnp.bfloat16)

def slot_tables(channel_order, owner_count, channel_good, capacity):
    starts = jnp.cumsum(owner_count) - owner_count
    positions = jnp.arange(capacity, dtype=jnp.int32)
    filled = positions[None, :] < owner_count[:, None]
    picked = jnp.minimum(starts[:, None] + positions[None, :], NCH - 1)
    channel = jnp.where(filled, channel_order[picked], 0).reshape(-1)
    slot_live = jnp.where(filled.reshape(-1), channel_good[channel], 0)
    return (channel, slot_live)

def block_spectra(block_volts, window, normalizer, table):
    as_float = block_volts.astype(jnp.float32)
    zeros_head = jnp.zeros((block_volts.shape[0], TAPS - 1, NSAMP), jnp.float32)
    padded = jnp.concatenate([zeros_head, as_float], axis=1)
    filtered = jnp.zeros_like(as_float)
    for k in range(TAPS):
        filtered = filtered + window[k] * padded[:, k:k + FRAMES]
    filtered = filtered.astype(jnp.bfloat16).reshape(BW * FRAMES, NSAMP)
    product = jnp.dot(filtered, table.reshape(NSAMP, NCH * 2), preferred_element_type=jnp.float32)
    spectrum = (product * normalizer).astype(jnp.bfloat16).reshape(BW, FRAMES, NCH, 2)
    return spectrum.transpose(3, 0, 1, 2)

def reference(voltages, channel_order, owner_count, channel_good):
    window, normalizer = pfb_window()
    table = transform_table()
    input_blocks = voltages.reshape(N_FREQ, BW, FRAMES, NSAMP)
    spectra = lax.map(lambda b: block_spectra(b, window, normalizer, table), input_blocks)
    channel, slot_live = slot_tables(channel_order, owner_count, channel_good, CAP)
    chosen = jnp.take(spectra, channel, axis=4)
    ordered = chosen.transpose(1, 3, 4, 0, 2).reshape(2, FRAMES, SLOTS, NINP)
    extended = jnp.concatenate([ordered, ordered[..., :HALF * BW]], axis=3)
    factor = slot_live.astype(jnp.float32) / FRAMES

    def row_block(block_index):
        left_side = lax.dynamic_slice_in_dim(extended, block_index * BW, BW, 3).astype(jnp.float32)
        right_side = lax.dynamic_slice_in_dim(extended, block_index * BW, HALF * BW, 3).astype(jnp.float32)
        real_sum = jnp.einsum('tmi,tmj->mij', left_side[0], right_side[0]) + jnp.einsum('tmi,tmj->mij', left_side[1], right_side[1])
        imag_sum = jnp.einsum('tmi,tmj->mij', left_side[1], right_side[0]) - jnp.einsum('tmi,tmj->mij', left_side[0], right_side[1])
        return (jnp.stack([real_sum, imag_sum]) * factor[None, :, None, None]).astype(jnp.bfloat16)
    row_blocks = lax.map(row_block, jnp.arange(N_FREQ, dtype=jnp.int32))
    return row_blocks.transpose(1, 2, 0, 3, 4).reshape(2, SLOTS, NINP, HALF * BW)
```

```python
import functools

import jax
import jax.numpy as jnp
import ml_dtypes
import numpy as np
from jax import lax
from jax.experimental import pallas as pl
from jax.experimental.pallas import tpu as pltpu
from jax.sharding import PartitionSpec as P

NSAMP = 2048
NCH = 512
TAPS = 4
CH0 = 256
MESH = pl.DeviceIdType.MESH


def shifted(value, axis, steps):
    count = lax.axis_size(axis)
    first, last = (max(0, -steps), min(count, count - steps))
    return lax.ppermute(value, axis, [(source, source + steps) for source in range(first, last)])


def pfb_window():
    offsets_u = np.arange(TAPS * NSAMP, dtype=np.float64)
    centered = (offsets_u - TAPS * NSAMP / 2) / NSAMP
    hann_taper = 0.5 - 0.5 * np.cos(2 * np.pi * offsets_u / (TAPS * NSAMP))
    window = (np.sinc(centered) * hann_taper).astype(np.float32).reshape(TAPS, NSAMP)
    normalizer = np.float32(1.0 / np.sqrt(np.sum(window.astype(np.float64) ** 2)))
    return (window, normalizer)


def transform_table():
    sample = np.arange(NSAMP, dtype=np.int64)
    channel_id = CH0 + np.arange(NCH, dtype=np.int64)
    angles = 2 * np.pi / NSAMP * (sample[None, :] * channel_id[:, None] % NSAMP)
    return np.stack([np.cos(angles), -np.sin(angles)], axis=0).astype(ml_dtypes.bfloat16)


def slot_tables(channel_order, owner_count, channel_good, capacity):
    starts = jnp.cumsum(owner_count) - owner_count
    positions = jnp.arange(capacity, dtype=jnp.int32)
    filled = positions[None, :] < owner_count[:, None]
    picked = jnp.minimum(starts[:, None] + positions[None, :], NCH - 1)
    channel = jnp.where(filled, channel_order[picked], 0).reshape(-1)
    slot_live = jnp.where(filled.reshape(-1), channel_good[channel], 0)
    return (channel, slot_live)


def exchange_kernel(cycle, owners, chunks, offsets, out_ref, buf_ref, local_sem, z_send, z_recv, f_send, f_recv):
    step_rows = out_ref.shape[1] // chunks
    me_f, me_z = lax.axis_index("freq"), lax.axis_index("blk")
    core = lax.rem(me_f, 2)
    side = lax.rem(me_f // 2, 2)
    mate_core = me_f + 1 - 2 * core
    mate_chip = me_f + 2 - 4 * side
    fours = [o for o in range(4, offsets, 4)]
    twos = [o for o in range(2, offsets, 4)]
    odds = [o for o in range(1, offsets, 2)]

    barrier = pltpu.get_barrier_semaphore()
    greeted = []
    for delta in range(1, owners):
        greeted.append((me_f, lax.rem(me_z + delta, owners)))
    far = sorted({o % cycle for o in fours} | {(cycle - o) % cycle for o in fours})
    for step in far:
        greeted.append((lax.rem(me_f + step, cycle), me_z))
    greeted.append((mate_core, me_z))
    greeted.append((mate_chip, me_z))
    for place in greeted:
        pl.semaphore_signal(barrier, inc=1, device_id=place, device_id_type=MESH)
    pl.semaphore_wait(barrier, len(greeted))

    def rows(c):
        return pl.ds(c * step_rows, step_rows)

    def own_copy(c):
        return pltpu.make_async_copy(
            out_ref.at[me_z, rows(c)], buf_ref.at[0, rows(c), me_z], local_sem.at[c]
        )

    def z_copy(c, delta):
        there = lax.rem(me_z + delta, owners)
        return pltpu.make_async_remote_copy(
            src_ref=out_ref.at[there, rows(c)],
            dst_ref=buf_ref.at[0, rows(c), me_z],
            send_sem=z_send.at[c, delta],
            recv_sem=z_recv.at[c, delta],
            device_id=(me_f, there),
            device_id_type=MESH,
        )

    def f_copy(c, o):
        if o % 4 == 0:
            held, there = 0, lax.rem(me_f + cycle - o, cycle)
        elif o % 4 == 2:
            held, there = o + 2 - 4 * side, mate_chip
        else:
            held, there = o + 1 - 2 * core, mate_core
        return pltpu.make_async_remote_copy(
            src_ref=buf_ref.at[held, rows(c)],
            dst_ref=buf_ref.at[o, rows(c)],
            send_sem=f_send.at[c, o],
            recv_sem=f_recv.at[c, o],
            device_id=(there, me_z),
            device_id_type=MESH,
        )

    @pl.loop(0, chunks)
    def _(c):
        own_copy(c).start()
        for delta in range(1, owners):
            z_copy(c, delta).start()

    @pl.loop(0, chunks + 2)
    def _(step):
        @pl.when(step < chunks)
        def _():
            own_copy(step).wait()
            for delta in range(1, owners):
                z_copy(step, delta).wait_recv()
            for o in fours:
                f_copy(step, o).start()

        @pl.when(jnp.logical_and(step >= 1, step < chunks + 1))
        def _():
            for o in fours:
                f_copy(step - 1, o).wait_recv()
            for o in twos:
                f_copy(step - 1, o).start()

        @pl.when(step >= 2)
        def _():
            for o in twos:
                f_copy(step - 2, o).wait_recv()
            for o in odds:
                f_copy(step - 2, o).start()

    @pl.loop(0, chunks)
    def _(c):
        for delta in range(1, owners):
            z_copy(c, delta).wait_send()
        for o in fours + twos:
            f_copy(c, o).wait_send()
        for o in odds:
            f_copy(c, o).wait()


def exchange(outgoing, cycle, owners, offsets, chunks):
    _, capacity, tile, width = outgoing.shape
    moved = outgoing.size * 2 * (1 + offsets)
    return pl.pallas_call(
        functools.partial(exchange_kernel, cycle, owners, chunks, offsets),
        out_shape=jax.ShapeDtypeStruct((offsets, capacity, owners, tile, width), outgoing.dtype),
        in_specs=[pl.BlockSpec(memory_space=pl.ANY)],
        out_specs=pl.BlockSpec(memory_space=pl.ANY),
        scratch_shapes=[
            pltpu.SemaphoreType.DMA((chunks,)),
            pltpu.SemaphoreType.DMA((chunks, owners)),
            pltpu.SemaphoreType.DMA((chunks, owners)),
            pltpu.SemaphoreType.DMA((chunks, offsets)),
            pltpu.SemaphoreType.DMA((chunks, offsets)),
        ],
        compiler_params=pltpu.CompilerParams(
            collective_id=0, has_side_effects=True, vmem_limit_bytes=16 * 1024 * 1024
        ),
        cost_estimate=pl.CostEstimate(flops=0, bytes_accessed=moved, transcendentals=0),
        name="exchange",
    )(outgoing)


def correlate_kernel(owners, factor_ref, spectra_ref, out_ref):
    offsets, slots, depth, width = spectra_ref.shape
    half = depth // (2 * owners)
    first = pl.program_id(0) * slots
    for m in range(slots):
        scale = factor_ref[first + m]
        own = spectra_ref[0, m]
        swapped = []
        for source in range(owners):
            low = source * 2 * half
            swapped.append(own[low + half : low + 2 * half])
            swapped.append(-own[low : low + half])
        turned = jnp.concatenate(swapped, axis=0)
        left = jnp.concatenate([own.T, turned.T], axis=0)
        for o in range(offsets):
            summed = jnp.dot(left, spectra_ref[o, m], preferred_element_type=jnp.float32) * scale
            summed = summed.astype(jnp.bfloat16)
            out_ref[0, m, :, o * width : (o + 1) * width] = summed[:width]
            out_ref[1, m, :, o * width : (o + 1) * width] = summed[width:]


def correlate(spectra, factor, owners, slots):
    offsets, capacity, depth, width = spectra.shape
    return pl.pallas_call(
        functools.partial(correlate_kernel, owners),
        grid=(capacity // slots,),
        out_shape=jax.ShapeDtypeStruct((2, capacity, width, offsets * width), jnp.bfloat16),
        in_specs=[
            pl.BlockSpec(memory_space=pltpu.SMEM),
            pl.BlockSpec((offsets, slots, depth, width), lambda g: (0, g, 0, 0)),
        ],
        out_specs=pl.BlockSpec((2, slots, width, offsets * width), lambda g: (0, g, 0, 0)),
        compiler_params=pltpu.CompilerParams(vmem_limit_bytes=48 * 1024 * 1024),
        cost_estimate=pl.CostEstimate(
            flops=4 * capacity * depth * width * width * offsets,
            bytes_accessed=2 * spectra.size + 4 * capacity * width * width * offsets,
            transcendentals=0,
        ),
        name="correlate",
    )(factor, spectra)


def body(voltages, channel_order, owner_count, channel_good):
    block_width, frame_count, sample_count = voltages.shape
    cycle_size = lax.axis_size("freq")
    owners = lax.axis_size("blk")
    capacity = 3 * NCH // (2 * owners)
    offset_count = cycle_size // 2 + 1
    frames_all = frame_count * owners
    window, normalizer = pfb_window()
    history = shifted(voltages[:, frame_count - (TAPS - 1) :, :], "blk", 1)
    padded = jnp.concatenate([history, voltages], axis=1)
    filtered = jnp.zeros((block_width, frame_count, sample_count), jnp.float32)
    for k in range(TAPS):
        filtered = filtered + window[k] * padded[:, k : k + frame_count].astype(jnp.float32)
    filtered = filtered.astype(jnp.bfloat16)
    spectra = jnp.einsum(
        "pcs,ifs->cpfi", transform_table(), filtered, preferred_element_type=jnp.float32
    )
    spectra = (spectra * normalizer).astype(jnp.bfloat16)
    channel, slot_live = slot_tables(channel_order, owner_count, channel_good, capacity)
    outgoing = jnp.take(spectra, channel, axis=0, mode="clip").reshape(
        owners, capacity, 2 * frame_count, block_width
    )
    chunks = max(1, capacity // 16)
    arrived = exchange(outgoing, cycle_size, owners, offset_count, chunks)
    arrived = arrived.reshape(offset_count, capacity, owners * 2 * frame_count, block_width)
    factor = (
        lax.dynamic_slice_in_dim(slot_live, lax.axis_index("blk") * capacity, capacity).astype(
            jnp.float32
        )
        / frames_all
    )
    return correlate(arrived, factor, owners, 8)


def solution(mesh):
    in_specs = (P("freq", "blk", None), P(), P(), P())
    out_specs = P(None, "blk", "freq", None)
    return jax.shard_map(body, mesh=mesh, in_specs=in_specs, out_specs=out_specs, check_vma=False)
```

```python
import functools

import jax
import jax.numpy as jnp
import ml_dtypes
import numpy as np
from jax import lax
from jax.experimental import pallas as pl
from jax.experimental.pallas import tpu as pltpu
from jax.sharding import PartitionSpec as P

NSAMP = 2048
NCH = 512
TAPS = 4
CH0 = 256
MESH = pl.DeviceIdType.MESH


def shifted(value, axis, steps):
    count = lax.axis_size(axis)
    first, last = (max(0, -steps), min(count, count - steps))
    return lax.ppermute(value, axis, [(source, source + steps) for source in range(first, last)])


def pfb_window():
    offsets_u = np.arange(TAPS * NSAMP, dtype=np.float64)
    centered = (offsets_u - TAPS * NSAMP / 2) / NSAMP
    hann_taper = 0.5 - 0.5 * np.cos(2 * np.pi * offsets_u / (TAPS * NSAMP))
    window = (np.sinc(centered) * hann_taper).astype(np.float32).reshape(TAPS, NSAMP)
    normalizer = np.float32(1.0 / np.sqrt(np.sum(window.astype(np.float64) ** 2)))
    return (window, normalizer)


def transform_table():
    sample = np.arange(NSAMP, dtype=np.int64)
    channel_id = CH0 + np.arange(NCH, dtype=np.int64)
    angles = 2 * np.pi / NSAMP * (sample[:, None] * channel_id[None, :] % NSAMP)
    return np.stack([np.cos(angles), -np.sin(angles)], axis=2).astype(ml_dtypes.bfloat16)


def slot_tables(channel_order, owner_count, channel_good, capacity):
    starts = jnp.cumsum(owner_count) - owner_count
    positions = jnp.arange(capacity, dtype=jnp.int32)
    filled = positions[None, :] < owner_count[:, None]
    picked = jnp.minimum(starts[:, None] + positions[None, :], NCH - 1)
    channel = jnp.where(filled, channel_order[picked], 0).reshape(-1)
    slot_live = jnp.where(filled.reshape(-1), channel_good[channel], 0)
    return (channel, slot_live)


def exchange_kernel(cycle, owners, chunks, offsets, out_ref, buf_ref, local_sem, z_send, z_recv, f_send, f_recv):
    step_rows = out_ref.shape[1] // chunks
    me_f, me_z = lax.axis_index("freq"), lax.axis_index("blk")
    core = lax.rem(me_f, 2)
    side = lax.rem(me_f // 2, 2)
    mate_core = me_f + 1 - 2 * core
    mate_chip = me_f + 2 - 4 * side
    fours = [o for o in range(4, offsets, 4)]
    twos = [o for o in range(2, offsets, 4)]
    odds = [o for o in range(1, offsets, 2)]

    barrier = pltpu.get_barrier_semaphore()
    greeted = []
    for delta in range(1, owners):
        greeted.append((me_f, lax.rem(me_z + delta, owners)))
    far = sorted({o % cycle for o in fours} | {(cycle - o) % cycle for o in fours})
    for step in far:
        greeted.append((lax.rem(me_f + step, cycle), me_z))
    greeted.append((mate_core, me_z))
    greeted.append((mate_chip, me_z))
    for place in greeted:
        pl.semaphore_signal(barrier, inc=1, device_id=place, device_id_type=MESH)
    pl.semaphore_wait(barrier, len(greeted))

    def rows(c):
        return pl.ds(c * step_rows, step_rows)

    def own_copy(c):
        return pltpu.make_async_copy(
            out_ref.at[me_z, rows(c)], buf_ref.at[0, rows(c), me_z], local_sem.at[c]
        )

    def z_copy(c, delta):
        there = lax.rem(me_z + delta, owners)
        return pltpu.make_async_remote_copy(
            src_ref=out_ref.at[there, rows(c)],
            dst_ref=buf_ref.at[0, rows(c), me_z],
            send_sem=z_send.at[c, delta],
            recv_sem=z_recv.at[c, delta],
            device_id=(me_f, there),
            device_id_type=MESH,
        )

    def f_copy(c, o):
        if o % 4 == 0:
            held, there = 0, lax.rem(me_f + cycle - o, cycle)
        elif o % 4 == 2:
            held, there = o + 2 - 4 * side, mate_chip
        else:
            held, there = o + 1 - 2 * core, mate_core
        return pltpu.make_async_remote_copy(
            src_ref=buf_ref.at[held, rows(c)],
            dst_ref=buf_ref.at[o, rows(c)],
            send_sem=f_send.at[c, o],
            recv_sem=f_recv.at[c, o],
            device_id=(there, me_z),
            device_id_type=MESH,
        )

    @pl.loop(0, chunks)
    def _(c):
        own_copy(c).start()
        for delta in range(1, owners):
            z_copy(c, delta).start()

    @pl.loop(0, chunks + 2)
    def _(step):
        @pl.when(step < chunks)
        def _():
            own_copy(step).wait()
            for delta in range(1, owners):
                z_copy(step, delta).wait_recv()
            for o in fours:
                f_copy(step, o).start()

        @pl.when(jnp.logical_and(step >= 1, step < chunks + 1))
        def _():
            for o in fours:
                f_copy(step - 1, o).wait_recv()
            for o in twos:
                f_copy(step - 1, o).start()

        @pl.when(step >= 2)
        def _():
            for o in twos:
                f_copy(step - 2, o).wait_recv()
            for o in odds:
                f_copy(step - 2, o).start()

    @pl.loop(0, chunks)
    def _(c):
        for delta in range(1, owners):
            z_copy(c, delta).wait_send()
        for o in fours + twos:
            f_copy(c, o).wait_send()
        for o in odds:
            f_copy(c, o).wait()


def exchange(outgoing, cycle, owners, offsets, chunks):
    _, capacity, tile, width = outgoing.shape
    moved = outgoing.size * 2 * (1 + offsets)
    return pl.pallas_call(
        functools.partial(exchange_kernel, cycle, owners, chunks, offsets),
        out_shape=jax.ShapeDtypeStruct((offsets, capacity, owners, tile, width), outgoing.dtype),
        in_specs=[pl.BlockSpec(memory_space=pl.ANY)],
        out_specs=pl.BlockSpec(memory_space=pl.ANY),
        scratch_shapes=[
            pltpu.SemaphoreType.DMA((chunks,)),
            pltpu.SemaphoreType.DMA((chunks, owners)),
            pltpu.SemaphoreType.DMA((chunks, owners)),
            pltpu.SemaphoreType.DMA((chunks, offsets)),
            pltpu.SemaphoreType.DMA((chunks, offsets)),
        ],
        compiler_params=pltpu.CompilerParams(
            collective_id=0, has_side_effects=True, vmem_limit_bytes=60 * 1024 * 1024
        ),
        cost_estimate=pl.CostEstimate(flops=0, bytes_accessed=moved, transcendentals=0),
        name="exchange",
    )(outgoing)


def correlate_kernel(owners, factor_ref, spectra_ref, out_ref):
    offsets, slots, depth, width = spectra_ref.shape
    half = depth // (2 * owners)
    first = pl.program_id(0) * slots
    for m in range(slots):
        scale = factor_ref[first + m]
        own = spectra_ref[0, m]
        swapped = []
        for source in range(owners):
            low = source * 2 * half
            swapped.append(own[low + half : low + 2 * half])
            swapped.append(-own[low : low + half])
        turned = jnp.concatenate(swapped, axis=0)
        left = jnp.concatenate([own.T, turned.T], axis=0)
        right = jnp.concatenate([spectra_ref[o, m] for o in range(offsets)], axis=1)
        summed = jnp.dot(left, right, preferred_element_type=jnp.float32) * scale
        summed = summed.astype(jnp.bfloat16)
        out_ref[0, m] = summed[:width]
        out_ref[1, m] = summed[width:]


def correlate(spectra, factor, owners, slots):
    offsets, capacity, depth, width = spectra.shape
    return pl.pallas_call(
        functools.partial(correlate_kernel, owners),
        grid=(capacity // slots,),
        out_shape=jax.ShapeDtypeStruct((2, capacity, width, offsets * width), jnp.bfloat16),
        in_specs=[
            pl.BlockSpec(memory_space=pltpu.SMEM),
            pl.BlockSpec((offsets, slots, depth, width), lambda g: (0, g, 0, 0)),
        ],
        out_specs=pl.BlockSpec((2, slots, width, offsets * width), lambda g: (0, g, 0, 0)),
        compiler_params=pltpu.CompilerParams(vmem_limit_bytes=48 * 1024 * 1024),
        cost_estimate=pl.CostEstimate(
            flops=4 * capacity * depth * width * width * offsets,
            bytes_accessed=2 * spectra.size + 4 * capacity * width * width * offsets,
            transcendentals=0,
        ),
        name="correlate",
    )(factor, spectra)


def body(voltages, channel_order, owner_count, channel_good):
    block_width, frame_count, sample_count = voltages.shape
    cycle_size = lax.axis_size("freq")
    owners = lax.axis_size("blk")
    capacity = 3 * NCH // (2 * owners)
    offset_count = cycle_size // 2 + 1
    frames_all = frame_count * owners
    window, normalizer = pfb_window()
    history = shifted(voltages[:, frame_count - (TAPS - 1) :, :], "blk", 1)
    padded = jnp.concatenate([history, voltages], axis=1)
    filtered = jnp.zeros((block_width, frame_count, sample_count), jnp.float32)
    for k in range(TAPS):
        filtered = filtered + window[k] * padded[:, k : k + frame_count].astype(jnp.float32)
    filtered = filtered.astype(jnp.bfloat16)
    spectra = jnp.einsum(
        "ifs,scp->fcpi", filtered, transform_table(), preferred_element_type=jnp.float32
    )
    spectra = lax.optimization_barrier((spectra * normalizer).astype(jnp.bfloat16))
    spectra = spectra.transpose(1, 2, 0, 3)
    channel, slot_live = slot_tables(channel_order, owner_count, channel_good, capacity)
    outgoing = jnp.take(spectra, channel, axis=0, mode="clip").reshape(
        owners, capacity, 2 * frame_count, block_width
    )
    chunks = max(1, capacity // 12)
    arrived = exchange(outgoing, cycle_size, owners, offset_count, chunks)
    arrived = arrived.reshape(offset_count, capacity, owners * 2 * frame_count, block_width)
    factor = (
        lax.dynamic_slice_in_dim(slot_live, lax.axis_index("blk") * capacity, capacity).astype(
            jnp.float32
        )
        / frames_all
    )
    return correlate(arrived, factor, owners, 8)


def solution(mesh):
    in_specs = (P("freq", "blk", None), P(), P(), P())
    out_specs = P(None, "blk", "freq", None)
    return jax.shard_map(body, mesh=mesh, in_specs=in_specs, out_specs=out_specs, check_vma=False)
```
